32 devices in a mesh: groups: 2 (over x), pts: 16 (over z, y, core).
Axes of the slice: x: 2, y: 2, z: 4, core: 2. Of those that a mesh axis runs over, the one named last changes fastest.
Arguments:
- occupied_at_nodes: bfloat16 [12288, 4096], P(('groups', 'pts')), parts along dimension 0, may hold values from -0.75 to 0.75
- within_group_screening: bfloat16 [12288, 384], P(('groups', 'pts')), parts along dimension 0, may hold values from -1.1953125 to 1.1953125
- adjacent_group_screening: bfloat16 [12288, 2, 384], P(('groups', 'pts')), parts along dimension 0, may hold values from -1.1953125 to 1.1953125
- close_couple_indicator: int32 [32, 2], P(('groups', 'pts')), parts along dimension 0, may hold values 0 or 1
- group_node_tally: int32 [32], P(('groups', 'pts')), parts along dimension 0, may hold values from 192 to 384, as said below
Outputs:
- exchange_rows: bfloat16 [12288, 4096], P(('groups', 'pts')), parts along dimension 0
The draws below stay inside these ranges and needn't reach their ends.
There are 2 independent parts, one for each index of `groups`. The reference program is written for one: setup_inputs(seed, part) draws one part's arguments, and reference() takes and returns one part's arrays. A program takes and returns all parts, laid end to end along the dimension named above; each array names one. Nothing has to cross between parts.
Inputs may be any that keep to these rules, and one draw needn't show every extreme that they name: `group_node_tally`: some block has all 384 points valid.
All inputs are finite; a program needn't handle non-finite values. No bound on the sum of `close_couple_indicator` on one device may be relied on, other than what follows from the above.
Results may differ from the reference program's by a relative error of at most 0.0051.
Values may be sent and summed in bfloat16 or wider, within the bound.
No kernel may reach another device: no remote copies, remote signals or barrier semaphores. Data moves between devices by JAX's collectives and lax.ppermute only.
A program may use at most 128 MiB of HBM per device.

```python
import jax
import jax.numpy as jnp
from jax import lax

PTS_DEV = 384
OCCUPIED_NUMBER = 4096
REACH = 2
NB = 16
NODE_NUMBER = 6144


def draw_group_node_tally(key, part):
    key = jax.random.fold_in(key, 11)
    first, second = jax.random.split(key)
    counts = jax.random.randint(first, (NB,), PTS_DEV // 2, PTS_DEV + 1)
    chosen = jax.random.randint(second, (), 0, NB)
    return jnp.where(jnp.arange(NB) == chosen, PTS_DEV, counts).astype(jnp.int32)


def touch_ends(entries, rng, least, top_value):
    longest = entries.shape.index(max(entries.shape))
    spots = []
    for shift in (0, 1):
        where = [jax.random.randint(jax.random.fold_in(rng, axis), (), 0, length) for axis, length in enumerate(entries.shape)]
        where[longest] = (where[longest] + shift) % entries.shape[longest]
        spots.append(tuple(where))
    return entries.at[spots[0]].set(least).at[spots[1]].set(top_value)


def levels(stream_key, extent, cuts, low, top_value):
    def one(axis_at, parts):
        heights = jax.random.uniform(jax.random.fold_in(jax.random.fold_in(stream_key, 6), axis_at), (parts,), jnp.float32, low / len(cuts), top_value / len(cuts))
        return jnp.repeat(jnp.exp(heights), extent[axis_at] // parts).reshape((-1,) + (1,) * (len(extent) - axis_at - 1))

    level = one(*cuts[0])
    for cut in cuts[1:]:
        level = level * one(*cut)
    return level


def centred(own_key, shape, deviation, bound, pieces=(), kind=jnp.bfloat16):
    result = jax.random.normal(own_key, shape, jnp.float32) * deviation
    if len(pieces) > 0:
        result = levels(own_key, shape, pieces, -0.22, 0.18) * result
    return jnp.clip(result, min=-bound, max=bound).astype(kind)


def setup_inputs(seed: int = 0, part: int = 0) -> dict:
    seeds = jax.random.split(jax.random.key(seed), 6)
    part_splits = jax.random.split(jax.random.fold_in(seeds[5], part), 6)
    return {
        "occupied_at_nodes": centred(part_splits[0], (NODE_NUMBER, OCCUPIED_NUMBER), 0.125, 0.75, ((0, 16),)),
        "within_group_screening": centred(part_splits[1], (NODE_NUMBER, PTS_DEV), 0.2, 1.1953125, ((0, 16),)),
        "adjacent_group_screening": centred(part_splits[2], (NODE_NUMBER, REACH, PTS_DEV), 0.2, 1.1953125, ((0, 16),)),
        "close_couple_indicator": touch_ends((jax.random.randint(part_splits[3], (NB, REACH), 0, 4) < 3).astype(jnp.int32), jax.random.fold_in(part_splits[3], 1), 0, 1),
        "group_node_tally": draw_group_node_tally(jax.random.fold_in(jax.random.fold_in(seeds[5], part), 71), part),
    }


def reference(occupied_at_nodes, within_group_screening, adjacent_group_screening, close_couple_indicator, group_node_tally):
    number_of_groupings = group_node_tally.shape[0]
    group_exchange_lines = within_group_screening.shape[1]
    occupied_function_samples = occupied_at_nodes.shape[1]
    node_locations = jnp.arange(group_exchange_lines, dtype=jnp.int32)
    usable_line_indicator = (node_locations[None, :] < group_node_tally[:, None]).astype(occupied_at_nodes.dtype)
    usable_nodes = occupied_at_nodes.reshape(number_of_groupings, group_exchange_lines, occupied_function_samples) * usable_line_indicator[:, :, None]
    cfull = usable_nodes.astype(jnp.float32)
    gram = jnp.einsum("bpn,bqn->bpq", cfull, cfull)
    kdiag = within_group_screening.reshape(number_of_groupings, group_exchange_lines, group_exchange_lines).astype(jnp.float32)
    wdiag = lax.optimization_barrier((kdiag * gram).astype(jnp.bfloat16)).astype(jnp.float32)
    total = jnp.einsum("bpq,bqn->bpn", wdiag, cfull)
    knear = adjacent_group_screening.reshape(number_of_groupings, group_exchange_lines, REACH, group_exchange_lines).astype(jnp.float32)
    for offset in range(1, REACH + 1):
        padding = jnp.zeros((offset, group_exchange_lines, occupied_function_samples), jnp.float32)
        above = jnp.concatenate([cfull[offset:], padding], axis=0)
        gram = jnp.einsum("bpn,bqn->bpq", cfull, above)
        pair_flag = close_couple_indicator[:, offset - 1].astype(jnp.float32)
        weights = knear[:, :, offset - 1, :] * gram * pair_flag[:, None, None]
        weights = lax.optimization_barrier(weights.astype(jnp.bfloat16)).astype(jnp.float32)
        total = total + jnp.einsum("bpq,bqn->bpn", weights, above)
        behind = jnp.einsum("bpq,bpn->bqn", weights, cfull)
        total = total + jnp.concatenate([padding, behind[:-offset]], axis=0)
    return (-total).reshape(number_of_groupings * group_exchange_lines, occupied_function_samples).astype(jnp.bfloat16)
```

```python
import jax
import jax.numpy as jnp
from jax import lax
from jax.sharding import PartitionSpec as P

CUTS = (96, 96, 96, 96)


def routes(peers):
    def pairs(f):
        return [(i, f(i)) for i in range(peers) if 0 <= f(i) < peers]

    across = pairs(lambda i: i ^ 2)
    onward = pairs(lambda i: i + 4 if (i // 2) % 2 == 0 else i - 4)
    sibling = pairs(lambda i: i ^ 1)
    return across, onward, sibling


def send(array, pairs):
    return lax.ppermute(array, "pts", pairs)


def stage(total, own, rows, kernel):
    gram = lax.dot_general(rows, own, (((1,), (1,)), ((), ())), preferred_element_type=jnp.float32)
    weights = (kernel.astype(jnp.float32) * gram).astype(jnp.bfloat16)
    part = lax.dot_general(weights, rows, (((0,), (0,)), ((), ())), preferred_element_type=jnp.float32)
    return part if total is None else total + part


def on_device(orbitals, kern_diag, kern_near, couple, tally):
    peers = lax.axis_size("pts")
    me = lax.axis_index("pts")
    odd_core = me % 2 == 1
    odd_chip = (me // 2) % 2 == 1
    across, onward, sibling = routes(peers)

    row = lax.iota(jnp.int32, orbitals.shape[0])
    valid = (row < tally[0]).astype(orbitals.dtype)
    own = orbitals * valid[:, None]

    flags = couple[0].astype(kern_near.dtype)
    near = [kern_near[:, o, :] * flags[o] for o in range(2)]
    below = [send(near[o], [(i, i + o + 1) for i in range(peers - o - 1)]) for o in range(2)]
    above = [n.T for n in near]
    k_sib = jnp.where(odd_core, below[0], above[0])
    k_swap = jnp.where(odd_core, above[0], below[0])
    k_across = jnp.where(odd_chip, below[1], above[1])
    k_onward = jnp.where(odd_chip, above[1], below[1])

    beside = send(own, sibling)
    total = stage(None, own, own, kern_diag.T)
    total = stage(total, own, beside, k_sib)
    at = 0
    for count in CUTS:
        rows = slice(at, at + count)
        from_across = send(own[rows], across)
        from_onward = send(from_across, onward)
        swapped = send(jnp.where(odd_core == odd_chip, from_across, from_onward), sibling)
        arrived = jnp.concatenate([from_across, from_onward, swapped])
        kernel = jnp.concatenate([k_across[rows], k_onward[rows], k_swap[rows]])
        total = stage(total, own, arrived, kernel)
        at += count
    return (-total).astype(jnp.bfloat16)


def solution(mesh):
    placed = (
        P(("groups", "pts"), None),
        P(("groups", "pts"), None),
        P(("groups", "pts"), None, None),
        P(("groups", "pts"), None),
        P(("groups", "pts")),
    )
    return jax.shard_map(
        on_device, mesh=mesh, in_specs=placed, out_specs=P(("groups", "pts"), None), check_vma=False
    )
```

```python
import functools

import jax
import jax.numpy as jnp
from jax import lax
from jax.experimental import pallas as pl
from jax.experimental.pallas import tpu as pltpu
from jax.sharding import PartitionSpec as P

CUTS = (64,) * 6
KAT = 5
LAG = 3
TILE = 512
MIB = 2**20


def routes(peers):
    def pairs(f):
        return [(i, f(i)) for i in range(peers) if 0 <= f(i) < peers]

    across = pairs(lambda i: i ^ 2)
    onward = pairs(lambda i: i + 4 if (i // 2) % 2 == 0 else i - 4)
    sibling = pairs(lambda i: i ^ 1)
    return across, onward, sibling


def send(array, pairs):
    return lax.ppermute(array, "pts", pairs)


def after(array, *gates):
    return lax.optimization_barrier((array, *gates))[0]


def grams(rows, own):
    return lax.dot_general(rows, own, (((1,), (1,)), ((), ())), preferred_element_type=jnp.float32)


def weigh(kern, gram):
    return kern.astype(jnp.float32) * gram


def tiles(width, body):
    def step(i, carry):
        body(pl.ds(pl.multiple_of(i * TILE, TILE), TILE))
        return carry

    lax.fori_loop(0, width // TILE, step, 0)


def call(body, out, args, scratch=(), smem=0, aliases=None, limit=16, flops=0):
    held = [pltpu.with_memory_space_constraint(a, pltpu.VMEM) for a in args[: len(args) - smem]]
    vector, scalar = pl.BlockSpec(memory_space=pltpu.VMEM), pl.BlockSpec(memory_space=pltpu.SMEM)
    return pl.pallas_call(
        body,
        out_shape=out,
        in_specs=[vector] * len(held) + [scalar] * smem,
        out_specs=jax.tree.map(lambda _: vector, out),
        input_output_aliases=aliases or {},
        scratch_shapes=list(scratch),
        compiler_params=pltpu.CompilerParams(vmem_limit_bytes=limit * MIB),
        cost_estimate=pl.CostEstimate(flops=flops, bytes_accessed=flops // 100, transcendentals=0),
    )(*held, *args[len(args) - smem :])


def prepare_body(near0, near1, couple, down0, down1, up0, up1):
    for o, (near, down, up) in enumerate(((near0, down0, up0), (near1, down1, up1))):
        kept = near[...].astype(jnp.float32) * couple[0, o].astype(jnp.float32)
        down[...] = kept.astype(down.dtype)
        up[...] = kept.T.astype(up.dtype)


def diagonal_body(own, kern, total, weights):
    weights[...] = weigh(kern[...], grams(own[...], own[...])).astype(weights.dtype)

    def tile(cols):
        total[:, cols] = jnp.dot(weights[...], own[:, cols], preferred_element_type=jnp.float32)

    tiles(own.shape[1], tile)


def collect_body(n, base, own, *refs):
    pieces, (rows, gram) = refs[:n], refs[-2:]
    at = base
    for piece in pieces:
        rows[at : at + piece.shape[0], :] = piece[...]
        at += piece.shape[0]
    gram[base:at, :] = grams(rows[base:at, :], own[...])


def pick(odd, down, up, rows):
    return jnp.where(odd, down[rows, :], up[rows, :])


def chosen(place, downs, ups, span):
    odd_core, odd_chip = (place & 1) == 1, (place & 2) == 2
    (down0, down1), (up0, up1) = downs, ups
    return [pick(odd_chip, down1, up1, span), pick(odd_chip, up1, down1, span), pick(odd_core, up0, down0, span)]


def product_body(spans, gram, rows, down0, down1, up0, up1, before, place, total, weights):
    odd_core = (place[0] & 1) == 1
    height = total.shape[0]
    kerns = [pick(odd_core, down0, up0, slice(0, height))]
    for span in spans:
        kerns += chosen(place[0], (down0, down1), (up0, up1), span)
    at = 0
    for kern in kerns:
        to = at + kern.shape[0]
        weights[at:to, :] = weigh(kern, gram[at:to, :]).astype(weights.dtype)
        at = to

    def tile(cols):
        part = lax.dot_general(
            weights[...], rows[:at, cols], (((0,), (0,)), ((), ())), preferred_element_type=jnp.float32
        )
        total[:, cols] = before[:, cols] + part

    tiles(total.shape[1], tile)


def last_body(span, own, across, onward, swap, down0, down1, up0, up1, before, place, out, rows, weights):
    at = 0
    for piece in (across, onward, swap):
        rows[at : at + piece.shape[0], :] = piece[...]
        at += piece.shape[0]
    kern = jnp.concatenate(chosen(place[0], (down0, down1), (up0, up1), span))
    weights[...] = weigh(kern, grams(rows[...], own[...])).T.astype(weights.dtype)

    def tile(cols):
        part = jnp.dot(weights[...], rows[:, cols], preferred_element_type=jnp.float32)
        out[:, cols] = (-(before[:, cols] + part)).astype(out.dtype)

    tiles(out.shape[1], tile)


def on_device(orbitals, kern_diag, kern_near, couple, tally):
    peers = lax.axis_size("pts")
    me = lax.axis_index("pts")
    mixed = ((me & 1) == 1) == ((me & 2) == 2)
    place = me.astype(jnp.int32)[None]
    across, onward, sibling = routes(peers)
    height, width = orbitals.shape
    kind = orbitals.dtype

    valid = (lax.iota(jnp.int32, height) < tally[0]).astype(kind)[:, None]
    spans, at = [], 0
    for count in CUTS:
        spans.append(slice(at, at + count))
        at += count
    last = len(spans) - 1

    held = {}

    def join(*names):
        names = [n for n in names if n in held]
        for n, value in zip(names, lax.optimization_barrier(tuple(held[n] for n in names))):
            held[n] = value

    def part(j, *gates):
        return after(orbitals, *gates)[spans[j]] * valid[spans[j]]

    def pieces(i):
        return [held["across", i], held["onward", i], held["swap", i]]

    first = part(0)
    held["across", 0] = send(first, across)
    second = part(1, first)
    held["across", 1] = send(second, across)
    own = after(orbitals, second) * valid
    beside = send(own, sibling)
    near = after(kern_near, own)
    square = jax.ShapeDtypeStruct((height, height), kind)
    down0, down1, up0, up1 = call(
        prepare_body, (square,) * 4, [near[:, 0, :], near[:, 1, :], couple], smem=1
    )
    held["total"] = call(
        diagonal_body, pltpu.VMEM((height, width), jnp.float32), [own, after(kern_diag, up0)],
        scratch=[pltpu.VMEM((height, height), kind)], flops=4 * height * height * width,
    )

    depth = height + 3 * (height - CUTS[-1])

    def collect(base, pieces):
        state = [held[n] for n in ("rows", "gram") if n in held]
        args = [own, *pieces] + state
        out = (pltpu.VMEM((depth, width), kind), pltpu.VMEM((depth, height), jnp.float32))
        aliases = {len(args) - 2: 0, len(args) - 1: 1} if state else {}
        count = sum(p.shape[0] for p in pieces)
        held["rows"], held["gram"] = call(
            functools.partial(collect_body, len(pieces), base), out, args, aliases=aliases,
            flops=2 * count * height * width,
        )

    collect(0, [after(beside, held["total"])])
    join(("across", 0), "rows", "gram")
    for w in range(1, last + 5):
        now = held["rows"]
        if w + 1 <= last:
            held["across", w + 1] = send(part(w + 1, now), across)
        if w - 1 <= last:
            held["onward", w - 1] = send(held["across", w - 1], onward)
        if w == KAT:
            for o, down in enumerate((down0, down1)):
                pairs = [(i, i + o + 1) for i in range(peers - o - 1)]
                held["down", o] = send(after(down, now), pairs)
        i = w - LAG
        if 0 <= i <= last:
            held["swap", i] = send(jnp.where(mixed, held["across", i], held["onward", i]), sibling)
        i -= 1
        if 0 <= i < last:
            collect(height + 3 * spans[i].start, pieces(i))
        if w <= last:
            join(("across", w), ("onward", w - LAG + 1), ("swap", w - LAG), "rows", "gram")
    downs = [held["down", o] for o in range(2)]
    state = held["rows"], held["gram"]
    total = held["total"]
    from_across, from_onward, swapped = ({last: piece} for piece in pieces(last))
    rows, gram = state
    kerns = [*downs, up0, up1]
    total = call(
        functools.partial(product_body, spans[:last]), pltpu.VMEM((height, width), jnp.float32),
        [gram, rows, *kerns, total, place], smem=1, aliases={6: 0},
        scratch=[pltpu.VMEM((depth, height), kind)], flops=2 * depth * height * width,
    )
    count = 3 * CUTS[-1]
    return call(
        functools.partial(last_body, spans[last]), jax.ShapeDtypeStruct((height, width), kind),
        [own, from_across[last], from_onward[last], swapped[last], *kerns, total, place], smem=1,
        scratch=[pltpu.VMEM((count, width), kind), pltpu.VMEM((height, count), kind)],
        flops=4 * count * height * width,
    )


def solution(mesh):
    placed = (
        P(("groups", "pts"), None),
        P(("groups", "pts"), None),
        P(("groups", "pts"), None, None),
        P(("groups", "pts"), None),
        P(("groups", "pts")),
    )
    return jax.shard_map(
        on_device, mesh=mesh, in_specs=placed, out_specs=P(("groups", "pts"), None), check_vma=False
    )
```

```python
import functools

import jax
import jax.numpy as jnp
from jax import lax
from jax.experimental import pallas as pl
from jax.experimental.pallas import tpu as pltpu
from jax.sharding import PartitionSpec as P

CUTS = (64,) * 6
KAT = 5
LAG = 3
HOLD = 2
TILE = 1024
MIB = 2**20


def routes(peers):
    def pairs(f):
        return [(i, f(i)) for i in range(peers) if 0 <= f(i) < peers]

    across = pairs(lambda i: i ^ 2)
    onward = pairs(lambda i: i + 4 if (i // 2) % 2 == 0 else i - 4)
    sibling = pairs(lambda i: i ^ 1)
    return across, onward, sibling


def send(array, pairs):
    return lax.ppermute(array, "pts", pairs)


def after(array, *gates):
    return lax.optimization_barrier((array, *gates))[0]


def grams(rows, own):
    return lax.dot_general(rows, own, (((1,), (1,)), ((), ())), preferred_element_type=jnp.float32)


def weigh(kern, gram):
    return kern.astype(jnp.float32) * gram


def tiles(width, body):
    def step(i, carry):
        body(pl.ds(pl.multiple_of(i * TILE, TILE), TILE))
        return carry

    lax.fori_loop(0, width // TILE, step, 0, unroll=True)


def call(body, out, args, scratch=(), smem=0, hbm=0, out_hbm=False, aliases=None, limit=16, flops=0):
    vectors = args[hbm : len(args) - smem]
    held = [*(pltpu.with_memory_space_constraint(a, pltpu.HBM) for a in args[:hbm]), *(pltpu.with_memory_space_constraint(a, pltpu.VMEM) for a in vectors)]
    vector, scalar = pl.BlockSpec(memory_space=pltpu.VMEM), pl.BlockSpec(memory_space=pltpu.SMEM)
    anywhere = pl.BlockSpec(memory_space=pl.ANY)
    return pl.pallas_call(
        body,
        out_shape=out,
        in_specs=[anywhere] * hbm + [vector] * len(vectors) + [scalar] * smem,
        out_specs=jax.tree.map(lambda _: anywhere if out_hbm else vector, out),
        input_output_aliases=aliases or {},
        scratch_shapes=list(scratch),
        compiler_params=pltpu.CompilerParams(vmem_limit_bytes=limit * MIB),
        cost_estimate=pl.CostEstimate(flops=flops, bytes_accessed=flops // 100, transcendentals=0),
    )(*held, *args[len(args) - smem :])


def prepare_body(near0, near1, couple, down0, down1, up0, up1):
    for o, (near, down, up) in enumerate(((near0, down0, up0), (near1, down1, up1))):
        kept = near[...].astype(jnp.float32) * couple[0, o].astype(jnp.float32)
        down[...] = kept.astype(down.dtype)
        up[...] = kept.T.astype(up.dtype)


def diagonal_body(own, kern, total, weights):
    weights[...] = weigh(kern[...], grams(own[...], own[...])).astype(weights.dtype)

    def tile(cols):
        total[:, cols] = jnp.dot(weights[...], own[:, cols], preferred_element_type=jnp.float32)

    tiles(own.shape[1], tile)


def collect_body(n, base, own, *refs):
    pieces, (rows, gram) = refs[:n], refs[-2:]
    at = base
    for piece in pieces:
        rows[at : at + piece.shape[0], :] = piece[...]
        at += piece.shape[0]
    gram[base:at, :] = grams(rows[base:at, :], own[...])


def pick(odd, down, up, rows):
    return jnp.where(odd, down[rows, :], up[rows, :])


def chosen(place, downs, ups, span):
    odd_core, odd_chip = (place & 1) == 1, (place & 2) == 2
    (down0, down1), (up0, up1) = downs, ups
    return [pick(odd_chip, down1, up1, span), pick(odd_chip, up1, down1, span), pick(odd_core, up0, down0, span)]


def product_body(spans, gram, rows, down0, down1, up0, up1, before, place, total, weights):
    odd_core = (place[0] & 1) == 1
    height = total.shape[0]
    kerns = [pick(odd_core, down0, up0, slice(0, height))]
    for span in spans:
        kerns += chosen(place[0], (down0, down1), (up0, up1), span)
    at = 0
    for kern in kerns:
        to = at + kern.shape[0]
        weights[at:to, :] = weigh(kern, gram[at:to, :]).astype(weights.dtype)
        at = to

    def tile(cols):
        part = lax.dot_general(
            weights[...], rows[:at, cols], (((0,), (0,)), ((), ())), preferred_element_type=jnp.float32
        )
        total[:, cols] = before[:, cols] + part

    tiles(total.shape[1], tile)


def last_body(span, n, own, *refs):
    pieces = refs[:n]
    down0, down1, up0, up1, before, place, out, rows, weights, ready, done = refs[n:]
    at = 0
    for piece in pieces:
        rows[at : at + piece.shape[0], :] = piece[...]
        at += piece.shape[0]
    kern = jnp.concatenate(chosen(place[0], (down0, down1), (up0, up1), span))
    weights[...] = weigh(kern, grams(rows[...], own[...])).T.astype(weights.dtype)
    copies = []
    for i in range(out.shape[1] // TILE):
        cols = slice(i * TILE, (i + 1) * TILE)
        part = jnp.dot(weights[...], rows[:, cols], preferred_element_type=jnp.float32)
        ready[:, cols] = (-(before[:, cols] + part)).astype(ready.dtype)
        copies.append(pltpu.make_async_copy(ready.at[:, cols], out.at[:, cols], done.at[i]))
        copies[-1].start()
    for copy in copies:
        copy.wait()


def on_device(orbitals, kern_diag, kern_near, couple, tally):
    peers = lax.axis_size("pts")
    me = lax.axis_index("pts")
    mixed = ((me & 1) == 1) == ((me & 2) == 2)
    place = me.astype(jnp.int32)[None]
    across, onward, sibling = routes(peers)
    height, width = orbitals.shape
    kind = orbitals.dtype

    valid = (lax.iota(jnp.int32, height) < tally[0]).astype(kind)[:, None]
    spans, at = [], 0
    for count in CUTS:
        spans.append(slice(at, at + count))
        at += count
    last = len(spans) - 1

    held = {}

    def join(*names):
        names = [n for n in names if n in held]
        for n, value in zip(names, lax.optimization_barrier(tuple(held[n] for n in names))):
            held[n] = value

    def part(j, *gates):
        return after(orbitals, *gates)[spans[j]] * valid[spans[j]]

    def pieces(i):
        return [held["across", i], held["onward", i], held["swap", i]]

    first = part(0)
    held["across", 0] = send(first, across)
    second = part(1, first)
    held["across", 1] = send(second, across)
    own = after(orbitals, second) * valid
    beside = send(own, sibling)
    near = after(kern_near, own)
    square = jax.ShapeDtypeStruct((height, height), kind)
    down0, down1, up0, up1 = call(
        prepare_body, (square,) * 4, [near[:, 0, :], near[:, 1, :], couple], smem=1
    )
    held["total"] = call(
        diagonal_body, pltpu.VMEM((height, width), jnp.float32), [own, after(kern_diag, up0)],
        scratch=[pltpu.VMEM((height, height), kind)], flops=4 * height * height * width,
    )

    depth = height + 3 * (height - sum(CUTS[-HOLD:]))

    def collect(base, pieces):
        state = [held[n] for n in ("rows", "gram") if n in held]
        args = [own, *pieces] + state
        out = (pltpu.VMEM((depth, width), kind), pltpu.VMEM((depth, height), jnp.float32))
        aliases = {len(args) - 2: 0, len(args) - 1: 1} if state else {}
        count = sum(p.shape[0] for p in pieces)
        held["rows"], held["gram"] = call(
            functools.partial(collect_body, len(pieces), base), out, args, aliases=aliases,
            flops=2 * count * height * width,
        )

    collect(0, [after(beside, held["total"])])
    join(("across", 0), "rows", "gram")
    def swap(i):
        held["swap", i] = send(jnp.where(mixed, held["across", i], held["onward", i]), sibling)

    def collected(i):
        collect(height + 3 * spans[i].start, pieces(i))

    swaps = collects = 0
    for w in range(1, last + 1):
        now = held["rows"]
        if w + 1 <= last:
            held["across", w + 1] = send(part(w + 1, now), across)
        held["onward", w - 1] = send(held["across", w - 1], onward)
        if w == KAT:
            for o, down in enumerate((down0, down1)):
                pairs = [(i, i + o + 1) for i in range(peers - o - 1)]
                held["down", o] = send(after(down, now), pairs)
        if w >= LAG:
            swap(w - LAG)
        if w >= LAG + 1:
            collected(w - LAG - 1)
        join(("across", w), ("onward", w - LAG + 1), ("swap", w - LAG), "rows", "gram")
    held["onward", last] = send(held["across", last], onward)
    if KAT > last:
        for o, down in enumerate((down0, down1)):
            pairs = [(i, i + o + 1) for i in range(peers - o - 1)]
            held["down", o] = send(after(down, held["rows"]), pairs)
    kept = last + 1 - HOLD
    for i in range(last - LAG + 1, kept):
        swap(i)
    join(("onward", last - 1), "rows", "gram")
    for i in range(last - LAG, kept):
        collected(i)
    gate = [("onward", i) for i in range(kept, last + 1)]
    join(*gate, "rows", "gram", ("down", 0), ("down", 1))
    for i in range(kept, last + 1):
        swap(i)
    kerns = [held["down", 0], held["down", 1], up0, up1]
    held["total"] = call(
        functools.partial(product_body, spans[:kept]), pltpu.VMEM((height, width), jnp.float32),
        [held["gram"], held["rows"], *kerns, held["total"], place], smem=1, aliases={6: 0},
        scratch=[pltpu.VMEM((depth, height), kind)], flops=2 * depth * height * width,
    )
    count = 3 * (height - spans[kept].start)
    final = [held[n, i] for n in ("across", "onward", "swap") for i in range(kept, last + 1)]
    return call(
        functools.partial(last_body, slice(spans[kept].start, height), len(final)),
        jax.ShapeDtypeStruct((height, width), kind),
        [own, *final, *kerns, held["total"], place], smem=1, out_hbm=True,
        scratch=[
            pltpu.VMEM((count, width), kind), pltpu.VMEM((height, count), kind), pltpu.VMEM((height, width), kind),
            pltpu.SemaphoreType.DMA((width // TILE,)),
        ],
        limit=16, flops=4 * count * height * width,
    )


def solution(mesh):
    placed = (
        P(("groups", "pts"), None),
        P(("groups", "pts"), None),
        P(("groups", "pts"), None, None),
        P(("groups", "pts"), None),
        P(("groups", "pts")),
    )
    return jax.shard_map(
        on_device, mesh=mesh, in_specs=placed, out_specs=P(("groups", "pts"), None), check_vma=False
    )
```

```python
import functools

import jax
import jax.numpy as jnp
from jax import lax
from jax.experimental import pallas as pl
from jax.experimental.pallas import tpu as pltpu
from jax.sharding import PartitionSpec as P

CUTS = (64,) * 6
KAT = 5
LAG = 3
HOLD = 2
TILE = 1024
SURE = 192
MIB = 2**20


def routes(peers):
    def pairs(f):
        return [(i, f(i)) for i in range(peers) if 0 <= f(i) < peers]

    across = pairs(lambda i: i ^ 2)
    onward = pairs(lambda i: i + 4 if (i // 2) % 2 == 0 else i - 4)
    sibling = pairs(lambda i: i ^ 1)
    return across, onward, sibling


def send(array, pairs):
    return lax.ppermute(array, "pts", pairs)


def after(array, *gates):
    return lax.optimization_barrier((array, *gates))[0]


def grams(rows, own):
    return lax.dot_general(rows, own, (((1,), (1,)), ((), ())), preferred_element_type=jnp.float32)


def weigh(kern, gram):
    return kern.astype(jnp.float32) * gram


def tiles(width, body):
    def step(i, carry):
        body(pl.ds(pl.multiple_of(i * TILE, TILE), TILE))
        return carry

    lax.fori_loop(0, width // TILE, step, 0, unroll=True)


def call(body, out, args, scratch=(), smem=0, hbm=0, out_hbm=False, aliases=None, limit=16, flops=0):
    vectors = args[hbm : len(args) - smem]
    held = [*(pltpu.with_memory_space_constraint(a, pltpu.HBM) for a in args[:hbm]), *(pltpu.with_memory_space_constraint(a, pltpu.VMEM) for a in vectors)]
    vector, scalar = pl.BlockSpec(memory_space=pltpu.VMEM), pl.BlockSpec(memory_space=pltpu.SMEM)
    anywhere = pl.BlockSpec(memory_space=pl.ANY)
    return pl.pallas_call(
        body,
        out_shape=out,
        in_specs=[anywhere] * hbm + [vector] * len(vectors) + [scalar] * smem,
        out_specs=jax.tree.map(lambda _: anywhere if out_hbm else vector, out),
        input_output_aliases=aliases or {},
        scratch_shapes=list(scratch),
        compiler_params=pltpu.CompilerParams(vmem_limit_bytes=limit * MIB),
        cost_estimate=pl.CostEstimate(flops=flops, bytes_accessed=flops // 100, transcendentals=0),
    )(*held, *args[len(args) - smem :])


def prepare_body(near0, near1, couple, down0, down1, up0, up1):
    for o, (near, down, up) in enumerate(((near0, down0, up0), (near1, down1, up1))):
        kept = near[...].astype(jnp.float32) * couple[0, o].astype(jnp.float32)
        down[...] = kept.astype(down.dtype)
        up[...] = kept.T.astype(up.dtype)


def diagonal_body(own, kern, total, weights):
    weights[...] = weigh(kern[...], grams(own[...], own[...])).astype(weights.dtype)

    def tile(cols):
        total[:, cols] = jnp.dot(weights[...], own[:, cols], preferred_element_type=jnp.float32)

    tiles(own.shape[1], tile)


def collect_body(n, base, own, *refs):
    pieces, (rows, gram) = refs[:n], refs[-2:]
    at = base
    for piece in pieces:
        rows[at : at + piece.shape[0], :] = piece[...]
        at += piece.shape[0]
    gram[base:at, :] = grams(rows[base:at, :], own[...])


def pick(odd, down, up, rows):
    return jnp.where(odd, down[rows, :], up[rows, :])


def chosen(place, downs, ups, span):
    odd_core, odd_chip = (place & 1) == 1, (place & 2) == 2
    (down0, down1), (up0, up1) = downs, ups
    return [pick(odd_chip, down1, up1, span), pick(odd_chip, up1, down1, span), pick(odd_core, up0, down0, span)]


def product_body(spans, gram, rows, down0, down1, up0, up1, before, place, total, weights):
    odd_core = (place[0] & 1) == 1
    height = total.shape[0]
    kerns = [pick(odd_core, down0, up0, slice(0, height))]
    for span in spans:
        kerns += chosen(place[0], (down0, down1), (up0, up1), span)
    at = 0
    for kern in kerns:
        to = at + kern.shape[0]
        weights[at:to, :] = weigh(kern, gram[at:to, :]).astype(weights.dtype)
        at = to

    def tile(cols):
        part = lax.dot_general(
            weights[...], rows[:at, cols], (((0,), (0,)), ((), ())), preferred_element_type=jnp.float32
        )
        total[:, cols] = before[:, cols] + part

    tiles(total.shape[1], tile)


def last_body(span, n, own, *refs):
    pieces = refs[:n]
    down0, down1, up0, up1, before, place, out, rows, weights, ready, done = refs[n:]
    at = 0
    for piece in pieces:
        rows[at : at + piece.shape[0], :] = piece[...]
        at += piece.shape[0]
    kern = jnp.concatenate(chosen(place[0], (down0, down1), (up0, up1), span))
    weights[...] = weigh(kern, grams(rows[...], own[...])).T.astype(weights.dtype)
    copies = []
    for i in range(out.shape[1] // TILE):
        cols = slice(i * TILE, (i + 1) * TILE)
        part = jnp.dot(weights[...], rows[:, cols], preferred_element_type=jnp.float32)
        ready[:, cols] = (-(before[:, cols] + part)).astype(ready.dtype)
        copies.append(pltpu.make_async_copy(ready.at[:, cols], out.at[:, cols], done.at[i]))
        copies[-1].start()
    for copy in copies:
        copy.wait()


def begin_body(spans, orbitals, tally, own, *refs):
    pieces, done = refs[:-1], refs[-1]
    head = sum(piece.shape[0] for piece in pieces)
    top = pltpu.make_async_copy(orbitals.at[:head], own.at[:head], done.at[0])
    rest = pltpu.make_async_copy(orbitals.at[head:], own.at[head:], done.at[1])
    top.start()
    rest.start()
    top.wait()
    copies = [pltpu.make_async_copy(own.at[span], piece, done.at[i + 2]) for i, (piece, span) in enumerate(zip(pieces, spans))]
    for copy in copies:
        copy.start()
    rest.wait()
    height, width = own.shape
    row = lax.broadcasted_iota(jnp.int32, (height - SURE, width), 0) + SURE
    own[SURE:, :] = jnp.where(row < tally[0], own[SURE:, :], jnp.zeros((), own.dtype))
    for copy in copies:
        copy.wait()


def on_device(orbitals, kern_diag, kern_near, couple, tally):
    peers = lax.axis_size("pts")
    me = lax.axis_index("pts")
    mixed = ((me & 1) == 1) == ((me & 2) == 2)
    place = me.astype(jnp.int32)[None]
    across, onward, sibling = routes(peers)
    height, width = orbitals.shape
    kind = orbitals.dtype

    valid = (lax.iota(jnp.int32, height) < tally[0]).astype(kind)[:, None]
    spans, at = [], 0
    for count in CUTS:
        spans.append(slice(at, at + count))
        at += count
    last = len(spans) - 1

    held = {}

    def join(*names):
        names = [n for n in names if n in held]
        for n, value in zip(names, lax.optimization_barrier(tuple(held[n] for n in names))):
            held[n] = value

    def part(j, *gates):
        return after(own, *gates)[spans[j]]

    def pieces(i):
        return [held["across", i], held["onward", i], held["swap", i]]

    begun = [pltpu.HBM((CUTS[j], width), kind) for j in range(2)]
    own, first, second = pl.pallas_call(
        functools.partial(begin_body, spans[:2]),
        out_shape=(pltpu.VMEM((height, width), kind), *begun),
        in_specs=[pl.BlockSpec(memory_space=pltpu.HBM), pl.BlockSpec(memory_space=pltpu.SMEM)],
        out_specs=(pl.BlockSpec(memory_space=pltpu.VMEM),) + (pl.BlockSpec(memory_space=pltpu.HBM),) * 2,
        scratch_shapes=[pltpu.SemaphoreType.DMA((4,))],
        compiler_params=pltpu.CompilerParams(vmem_limit_bytes=8 * MIB),
    )(pltpu.with_memory_space_constraint(orbitals, pltpu.HBM), tally)
    held["across", 0] = send(first, across)
    held["across", 1] = send(second, across)
    beside = send(own, sibling)
    near = after(kern_near, own)
    square = jax.ShapeDtypeStruct((height, height), kind)
    down0, down1, up0, up1 = call(
        prepare_body, (square,) * 4, [near[:, 0, :], near[:, 1, :], couple], smem=1
    )
    held["total"] = call(
        diagonal_body, pltpu.VMEM((height, width), jnp.float32), [own, after(kern_diag, up0)],
        scratch=[pltpu.VMEM((height, height), kind)], flops=4 * height * height * width,
    )

    depth = height + 3 * (height - sum(CUTS[-HOLD:]))

    def collect(base, pieces):
        state = [held[n] for n in ("rows", "gram") if n in held]
        args = [own, *pieces] + state
        out = (pltpu.VMEM((depth, width), kind), pltpu.VMEM((depth, height), jnp.float32))
        aliases = {len(args) - 2: 0, len(args) - 1: 1} if state else {}
        count = sum(p.shape[0] for p in pieces)
        held["rows"], held["gram"] = call(
            functools.partial(collect_body, len(pieces), base), out, args, aliases=aliases,
            flops=2 * count * height * width,
        )

    join(("across", 0), "total")
    def swap(i):
        held["swap", i] = send(jnp.where(mixed, held["across", i], held["onward", i]), sibling)

    def collected(i):
        collect(height + 3 * spans[i].start, pieces(i))

    swaps = collects = 0
    for w in range(1, last + 1):
        now = held["total"]
        if w + 1 <= last:
            held["across", w + 1] = send(part(w + 1, now), across)
        held["onward", w - 1] = send(held["across", w - 1], onward)
        if w == KAT:
            for o, down in enumerate((down0, down1)):
                pairs = [(i, i + o + 1) for i in range(peers - o - 1)]
                held["down", o] = send(after(down, now), pairs)
        if w >= LAG:
            swap(w - LAG)
        if w == LAG:
            collect(0, [after(beside, held["total"])])
        if w >= LAG + 1:
            collected(w - LAG - 1)
        join(("across", w), ("onward", w - LAG + 1), ("swap", w - LAG), "rows", "gram", "total")
    held["onward", last] = send(held["across", last], onward)
    if KAT > last:
        for o, down in enumerate((down0, down1)):
            pairs = [(i, i + o + 1) for i in range(peers - o - 1)]
            held["down", o] = send(after(down, held["rows"]), pairs)
    kept = last + 1 - HOLD
    for i in range(last - LAG + 1, kept):
        swap(i)
    join(("onward", last - 1), "rows", "gram")
    for i in range(last - LAG, kept):
        collected(i)
    gate = [("onward", i) for i in range(kept, last + 1)]
    join(*gate, "rows", "gram", ("down", 0), ("down", 1))
    for i in range(kept, last + 1):
        swap(i)
    kerns = [held["down", 0], held["down", 1], up0, up1]
    held["total"] = call(
        functools.partial(product_body, spans[:kept]), pltpu.VMEM((height, width), jnp.float32),
        [held["gram"], held["rows"], *kerns, held["total"], place], smem=1, aliases={6: 0},
        scratch=[pltpu.VMEM((depth, height), kind)], flops=2 * depth * height * width,
    )
    count = 3 * (height - spans[kept].start)
    final = [held[n, i] for n in ("across", "onward", "swap") for i in range(kept, last + 1)]
    return call(
        functools.partial(last_body, slice(spans[kept].start, height), len(final)),
        jax.ShapeDtypeStruct((height, width), kind),
        [own, *final, *kerns, held["total"], place], smem=1, out_hbm=True,
        scratch=[
            pltpu.VMEM((count, width), kind), pltpu.VMEM((height, count), kind), pltpu.VMEM((height, width), kind),
            pltpu.SemaphoreType.DMA((width // TILE,)),
        ],
        limit=16, flops=4 * count * height * width,
    )


def solution(mesh):
    placed = (
        P(("groups", "pts"), None),
        P(("groups", "pts"), None),
        P(("groups", "pts"), None, None),
        P(("groups", "pts"), None),
        P(("groups", "pts")),
    )
    return jax.shard_map(
        on_device, mesh=mesh, in_specs=placed, out_specs=P(("groups", "pts"), None), check_vma=False
    )
```

```python
import functools

import jax
import jax.numpy as jnp
from jax import lax
from jax.experimental import pallas as pl
from jax.experimental.pallas import tpu as pltpu
from jax.sharding import PartitionSpec as P

CUTS = (48,) * 8
KAT = 7
LAG = 3
HOLD = 2
TILE = 1024
SURE = 192
MIB = 2**20


def routes(peers):
    def pairs(f):
        return [(i, f(i)) for i in range(peers) if 0 <= f(i) < peers]

    across = pairs(lambda i: i ^ 2)
    onward = pairs(lambda i: i + 4 if (i // 2) % 2 == 0 else i - 4)
    sibling = pairs(lambda i: i ^ 1)
    return across, onward, sibling


def send(array, pairs):
    return lax.ppermute(array, "pts", pairs)


def after(array, *gates):
    return lax.optimization_barrier((array, *gates))[0]


def grams(rows, own):
    return lax.dot_general(rows, own, (((1,), (1,)), ((), ())), preferred_element_type=jnp.float32)


def weigh(kern, gram):
    return kern.astype(jnp.float32) * gram


def tiles(width, body):
    def step(i, carry):
        body(pl.ds(pl.multiple_of(i * TILE, TILE), TILE))
        return carry

    lax.fori_loop(0, width // TILE, step, 0, unroll=True)


def call(body, out, args, scratch=(), smem=0, hbm=0, out_hbm=False, aliases=None, limit=16, flops=0):
    vectors = args[hbm : len(args) - smem]
    held = [*(pltpu.with_memory_space_constraint(a, pltpu.HBM) for a in args[:hbm]), *(pltpu.with_memory_space_constraint(a, pltpu.VMEM) for a in vectors)]
    vector, scalar = pl.BlockSpec(memory_space=pltpu.VMEM), pl.BlockSpec(memory_space=pltpu.SMEM)
    anywhere = pl.BlockSpec(memory_space=pl.ANY)
    return pl.pallas_call(
        body,
        out_shape=out,
        in_specs=[anywhere] * hbm + [vector] * len(vectors) + [scalar] * smem,
        out_specs=jax.tree.map(lambda _: anywhere if out_hbm else vector, out),
        input_output_aliases=aliases or {},
        scratch_shapes=list(scratch),
        compiler_params=pltpu.CompilerParams(vmem_limit_bytes=limit * MIB),
        cost_estimate=pl.CostEstimate(flops=flops, bytes_accessed=flops // 100, transcendentals=0),
    )(*held, *args[len(args) - smem :])


def prepare_body(near0, near1, couple, down0, down1, up0, up1):
    for o, (near, down, up) in enumerate(((near0, down0, up0), (near1, down1, up1))):
        kept = near[...].astype(jnp.float32) * couple[0, o].astype(jnp.float32)
        down[...] = kept.astype(down.dtype)
        up[...] = kept.T.astype(up.dtype)


def diagonal_body(own, kern, total, weights):
    weights[...] = weigh(kern[...], grams(own[...], own[...])).astype(weights.dtype)

    def tile(cols):
        total[:, cols] = jnp.dot(weights[...], own[:, cols], preferred_element_type=jnp.float32)

    tiles(own.shape[1], tile)


def collect_body(n, base, own, *refs):
    pieces, (rows, gram) = refs[:n], refs[-2:]
    at = base
    for piece in pieces:
        rows[at : at + piece.shape[0], :] = piece[...]
        at += piece.shape[0]
    gram[base:at, :] = grams(rows[base:at, :], own[...])


def pick(odd, down, up, rows):
    return jnp.where(odd, down[rows, :], up[rows, :])


def chosen(place, downs, ups, span):
    odd_core, odd_chip = (place & 1) == 1, (place & 2) == 2
    (down0, down1), (up0, up1) = downs, ups
    return [pick(odd_chip, down1, up1, span), pick(odd_chip, up1, down1, span), pick(odd_core, up0, down0, span)]


def product_body(spans, gram, rows, down0, down1, up0, up1, before, place, total, weights):
    odd_core = (place[0] & 1) == 1
    height = total.shape[0]
    kerns = [pick(odd_core, down0, up0, slice(0, height))]
    for span in spans:
        kerns += chosen(place[0], (down0, down1), (up0, up1), span)
    at = 0
    for kern in kerns:
        to = at + kern.shape[0]
        weights[at:to, :] = weigh(kern, gram[at:to, :]).astype(weights.dtype)
        at = to

    def tile(cols):
        part = lax.dot_general(
            weights[...], rows[:at, cols], (((0,), (0,)), ((), ())), preferred_element_type=jnp.float32
        )
        total[:, cols] = before[:, cols] + part

    tiles(total.shape[1], tile)


def last_body(span, n, own, *refs):
    pieces = refs[:n]
    down0, down1, up0, up1, before, place, out, rows, weights, ready, done = refs[n:]
    at = 0
    for piece in pieces:
        rows[at : at + piece.shape[0], :] = piece[...]
        at += piece.shape[0]
    kern = jnp.concatenate(chosen(place[0], (down0, down1), (up0, up1), span))
    weights[...] = weigh(kern, grams(rows[...], own[...])).T.astype(weights.dtype)
    copies = []
    for i in range(out.shape[1] // TILE):
        cols = slice(i * TILE, (i + 1) * TILE)
        part = jnp.dot(weights[...], rows[:, cols], preferred_element_type=jnp.float32)
        ready[:, cols] = (-(before[:, cols] + part)).astype(ready.dtype)
        copies.append(pltpu.make_async_copy(ready.at[:, cols], out.at[:, cols], done.at[i]))
        copies[-1].start()
    for copy in copies:
        copy.wait()


def begin_body(spans, orbitals, tally, own, *refs):
    pieces, done = refs[:-1], refs[-1]
    head = sum(piece.shape[0] for piece in pieces)
    top = pltpu.make_async_copy(orbitals.at[:head], own.at[:head], done.at[0])
    rest = pltpu.make_async_copy(orbitals.at[head:], own.at[head:], done.at[1])
    top.start()
    rest.start()
    top.wait()
    copies = [pltpu.make_async_copy(own.at[span], piece, done.at[i + 2]) for i, (piece, span) in enumerate(zip(pieces, spans))]
    for copy in copies:
        copy.start()
    rest.wait()
    height, width = own.shape
    row = lax.broadcasted_iota(jnp.int32, (height - SURE, width), 0) + SURE
    own[SURE:, :] = jnp.where(row < tally[0], own[SURE:, :], jnp.zeros((), own.dtype))
    for copy in copies:
        copy.wait()


def on_device(orbitals, kern_diag, kern_near, couple, tally):
    peers = lax.axis_size("pts")
    me = lax.axis_index("pts")
    mixed = ((me & 1) == 1) == ((me & 2) == 2)
    place = me.astype(jnp.int32)[None]
    across, onward, sibling = routes(peers)
    height, width = orbitals.shape
    kind = orbitals.dtype

    valid = (lax.iota(jnp.int32, height) < tally[0]).astype(kind)[:, None]
    spans, at = [], 0
    for count in CUTS:
        spans.append(slice(at, at + count))
        at += count
    last = len(spans) - 1

    held = {}

    def join(*names):
        names = [n for n in names if n in held]
        for n, value in zip(names, lax.optimization_barrier(tuple(held[n] for n in names))):
            held[n] = value

    def part(j, *gates):
        return after(own, *gates)[spans[j]]

    def pieces(i):
        return [held["across", i], held["onward", i], held["swap", i]]

    begun = [pltpu.HBM((CUTS[j], width), kind) for j in range(2)]
    own, first, second = pl.pallas_call(
        functools.partial(begin_body, spans[:2]),
        out_shape=(pltpu.VMEM((height, width), kind), *begun),
        in_specs=[pl.BlockSpec(memory_space=pltpu.HBM), pl.BlockSpec(memory_space=pltpu.SMEM)],
        out_specs=(pl.BlockSpec(memory_space=pltpu.VMEM),) + (pl.BlockSpec(memory_space=pltpu.HBM),) * 2,
        scratch_shapes=[pltpu.SemaphoreType.DMA((4,))],
        compiler_params=pltpu.CompilerParams(vmem_limit_bytes=8 * MIB),
    )(pltpu.with_memory_space_constraint(orbitals, pltpu.HBM), tally)
    held["across", 0] = send(first, across)
    held["across", 1] = send(second, across)
    beside = send(own, sibling)
    near = after(kern_near, own)
    square = jax.ShapeDtypeStruct((height, height), kind)
    down0, down1, up0, up1 = call(
        prepare_body, (square,) * 4, [near[:, 0, :], near[:, 1, :], couple], smem=1
    )
    held["total"] = call(
        diagonal_body, pltpu.VMEM((height, width), jnp.float32), [own, after(kern_diag, up0)],
        scratch=[pltpu.VMEM((height, height), kind)], flops=4 * height * height * width,
    )

    depth = height + 3 * (height - sum(CUTS[-HOLD:]))

    def collect(base, pieces):
        state = [held[n] for n in ("rows", "gram") if n in held]
        args = [own, *pieces] + state
        out = (pltpu.VMEM((depth, width), kind), pltpu.VMEM((depth, height), jnp.float32))
        aliases = {len(args) - 2: 0, len(args) - 1: 1} if state else {}
        count = sum(p.shape[0] for p in pieces)
        held["rows"], held["gram"] = call(
            functools.partial(collect_body, len(pieces), base), out, args, aliases=aliases,
            flops=2 * count * height * width,
        )

    join(("across", 0), "total")
    def swap(i):
        held["swap", i] = send(jnp.where(mixed, held["across", i], held["onward", i]), sibling)

    def collected(i):
        collect(height + 3 * spans[i].start, pieces(i))

    swaps = collects = 0
    for w in range(1, last + 1):
        now = held["total"]
        if w + 1 <= last:
            held["across", w + 1] = send(part(w + 1, now), across)
        held["onward", w - 1] = send(held["across", w - 1], onward)
        if w == KAT:
            for o, down in ((1, down1), (0, down0)):
                pairs = [(i, i + o + 1) for i in range(peers - o - 1)]
                held["down", o] = send(after(down, now), pairs)
        if w >= LAG:
            swap(w - LAG)
        if w == LAG:
            collect(0, [after(beside, held["total"])])
        if w >= LAG + 1:
            collected(w - LAG - 1)
        join(("across", w), ("onward", w - LAG + 1), ("swap", w - LAG), "rows", "gram", "total")
    held["onward", last] = send(held["across", last], onward)
    if KAT > last:
        for o, down in ((1, down1), (0, down0)):
            pairs = [(i, i + o + 1) for i in range(peers - o - 1)]
            held["down", o] = send(after(down, held["rows"]), pairs)
    kept = last + 1 - HOLD
    for i in range(last - LAG + 1, kept):
        swap(i)
    join(("onward", last - 1), "rows", "gram")
    for i in range(last - LAG, kept):
        collected(i)
    gate = [("onward", i) for i in range(kept, last + 1)]
    join(*gate, "rows", "gram", ("down", 0), ("down", 1))
    for i in range(kept, last + 1):
        swap(i)
    kerns = [held["down", 0], held["down", 1], up0, up1]
    held["total"] = call(
        functools.partial(product_body, spans[:kept]), pltpu.VMEM((height, width), jnp.float32),
        [held["gram"], held["rows"], *kerns, held["total"], place], smem=1, aliases={6: 0},
        scratch=[pltpu.VMEM((depth, height), kind)], flops=2 * depth * height * width,
    )
    count = 3 * (height - spans[kept].start)
    final = [held[n, i] for n in ("across", "onward", "swap") for i in range(kept, last + 1)]
    return call(
        functools.partial(last_body, slice(spans[kept].start, height), len(final)),
        jax.ShapeDtypeStruct((height, width), kind),
        [own, *final, *kerns, held["total"], place], smem=1, out_hbm=True,
        scratch=[
            pltpu.VMEM((count, width), kind), pltpu.VMEM((height, count), kind), pltpu.VMEM((height, width), kind),
            pltpu.SemaphoreType.DMA((width // TILE,)),
        ],
        limit=16, flops=4 * count * height * width,
    )


def solution(mesh):
    placed = (
        P(("groups", "pts"), None),
        P(("groups", "pts"), None),
        P(("groups", "pts"), None, None),
        P(("groups", "pts"), None),
        P(("groups", "pts")),
    )
    return jax.shard_map(
        on_device, mesh=mesh, in_specs=placed, out_specs=P(("groups", "pts"), None), check_vma=False
    )
```

```python
import functools

import jax
import jax.numpy as jnp
from jax import lax
from jax.experimental import pallas as pl
from jax.experimental.pallas import tpu as pltpu
from jax.sharding import PartitionSpec as P

CUTS = (48,) * 8
KAT = 7
LAG = 3
HOLD = 2
TILE = 1024
SURE = 192
MIB = 2**20


def routes(peers):
    def pairs(f):
        return [(i, f(i)) for i in range(peers) if 0 <= f(i) < peers]

    across = pairs(lambda i: i ^ 2)
    onward = pairs(lambda i: i + 4 if (i // 2) % 2 == 0 else i - 4)
    sibling = pairs(lambda i: i ^ 1)
    return across, onward, sibling


def send(array, pairs):
    return lax.ppermute(array, "pts", pairs)


def after(array, *gates):
    return lax.optimization_barrier((array, *gates))[0]


def grams(rows, own):
    return lax.dot_general(rows, own, (((1,), (1,)), ((), ())), preferred_element_type=jnp.float32)


def weigh(kern, gram):
    return kern.astype(jnp.float32) * gram


def tiles(width, body):
    def step(i, carry):
        body(pl.ds(pl.multiple_of(i * TILE, TILE), TILE))
        return carry

    lax.fori_loop(0, width // TILE, step, 0, unroll=True)


def call(body, out, args, scratch=(), smem=0, hbm=0, out_hbm=False, aliases=None, limit=16, flops=0):
    vectors = args[hbm : len(args) - smem]
    held = [*(pltpu.with_memory_space_constraint(a, pltpu.HBM) for a in args[:hbm]), *(pltpu.with_memory_space_constraint(a, pltpu.VMEM) for a in vectors)]
    vector, scalar = pl.BlockSpec(memory_space=pltpu.VMEM), pl.BlockSpec(memory_space=pltpu.SMEM)
    anywhere = pl.BlockSpec(memory_space=pl.ANY)
    return pl.pallas_call(
        body,
        out_shape=out,
        in_specs=[anywhere] * hbm + [vector] * len(vectors) + [scalar] * smem,
        out_specs=jax.tree.map(lambda _: anywhere if out_hbm else vector, out),
        input_output_aliases=aliases or {},
        scratch_shapes=list(scratch),
        compiler_params=pltpu.CompilerParams(vmem_limit_bytes=limit * MIB),
        cost_estimate=pl.CostEstimate(flops=flops, bytes_accessed=flops // 100, transcendentals=0),
    )(*held, *args[len(args) - smem :])


def prepare_body(near0, near1, couple, down0, down1, up0, up1):
    for o, (near, down, up) in enumerate(((near0, down0, up0), (near1, down1, up1))):
        kept = near[...].astype(jnp.float32) * couple[0, o].astype(jnp.float32)
        down[...] = kept.astype(down.dtype)
        up[...] = kept.T.astype(up.dtype)


def diagonal_body(own, kern, total, weights):
    weights[...] = weigh(kern[...], grams(own[...], own[...])).astype(weights.dtype)

    def tile(cols):
        total[:, cols] = jnp.dot(weights[...], own[:, cols], preferred_element_type=jnp.float32)

    tiles(own.shape[1], tile)


def collect_body(n, base, own, *refs):
    pieces, (rows, gram) = refs[:n], refs[-2:]
    at = base
    for piece in pieces:
        rows[at : at + piece.shape[0], :] = piece[...]
        at += piece.shape[0]
    gram[base:at, :] = grams(rows[base:at, :], own[...])


def pick(odd, down, up, rows):
    return jnp.where(odd, down[rows, :], up[rows, :])


def chosen(place, downs, ups, span):
    odd_core, odd_chip = (place & 1) == 1, (place & 2) == 2
    (down0, down1), (up0, up1) = downs, ups
    return [pick(odd_chip, down1, up1, span), pick(odd_chip, up1, down1, span), pick(odd_core, up0, down0, span)]


def product_body(spans, gram, rows, down0, down1, up0, up1, before, place, total, weights):
    odd_core = (place[0] & 1) == 1
    height = total.shape[0]
    kerns = [pick(odd_core, down0, up0, slice(0, height))]
    for span in spans:
        kerns += chosen(place[0], (down0, down1), (up0, up1), span)
    at = 0
    for kern in kerns:
        to = at + kern.shape[0]
        weights[at:to, :] = weigh(kern, gram[at:to, :]).astype(weights.dtype)
        at = to

    def tile(cols):
        part = lax.dot_general(
            weights[...], rows[:at, cols], (((0,), (0,)), ((), ())), preferred_element_type=jnp.float32
        )
        total[:, cols] = before[:, cols] + part

    tiles(total.shape[1], tile)


def last_body(span, n, own, *refs):
    pieces = refs[:n]
    down0, down1, up0, up1, before, place, out, rows, weights, ready, done = refs[n:]
    at = 0
    for piece in pieces:
        rows[at : at + piece.shape[0], :] = piece[...]
        at += piece.shape[0]
    kern = jnp.concatenate(chosen(place[0], (down0, down1), (up0, up1), span))
    weights[...] = weigh(kern, grams(rows[...], own[...])).T.astype(weights.dtype)
    copies = []
    for i in range(out.shape[1] // TILE):
        cols = slice(i * TILE, (i + 1) * TILE)
        part = jnp.dot(weights[...], rows[:, cols], preferred_element_type=jnp.float32)
        ready[:, cols] = (-(before[:, cols] + part)).astype(ready.dtype)
        copies.append(pltpu.make_async_copy(ready.at[:, cols], out.at[:, cols], done.at[i]))
        copies[-1].start()
    for copy in copies:
        copy.wait()


def begin_body(spans, orbitals, tally, own, *refs):
    pieces, done = refs[:-1], refs[-1]
    head = sum(piece.shape[0] for piece in pieces)
    top = pltpu.make_async_copy(orbitals.at[:head], own.at[:head], done.at[0])
    rest = pltpu.make_async_copy(orbitals.at[head:], own.at[head:], done.at[1])
    top.start()
    rest.start()
    top.wait()
    copies = [pltpu.make_async_copy(own.at[span], piece, done.at[i + 2]) for i, (piece, span) in enumerate(zip(pieces, spans))]
    for copy in copies:
        copy.start()
    rest.wait()
    height, width = own.shape
    row = lax.broadcasted_iota(jnp.int32, (height - SURE, width), 0) + SURE
    own[SURE:, :] = jnp.where(row < tally[0], own[SURE:, :], jnp.zeros((), own.dtype))
    for copy in copies:
        copy.wait()


def on_device(orbitals, kern_diag, kern_near, couple, tally):
    peers = lax.axis_size("pts")
    me = lax.axis_index("pts")
    mixed = ((me & 1) == 1) == ((me & 2) == 2)
    place = me.astype(jnp.int32)[None]
    across, onward, sibling = routes(peers)
    height, width = orbitals.shape
    kind = orbitals.dtype

    valid = (lax.iota(jnp.int32, height) < tally[0]).astype(kind)[:, None]
    spans, at = [], 0
    for count in CUTS:
        spans.append(slice(at, at + count))
        at += count
    last = len(spans) - 1

    held = {}

    def join(*names):
        names = [n for n in names if n in held]
        for n, value in zip(names, lax.optimization_barrier(tuple(held[n] for n in names))):
            held[n] = value

    def part(j, *gates):
        return after(own, *gates)[spans[j]]

    def pieces(i):
        return [held["across", i], held["onward", i], held["swap", i]]

    begun = [pltpu.HBM((CUTS[j], width), kind) for j in range(2)]
    own, first, second = pl.pallas_call(
        functools.partial(begin_body, spans[:2]),
        out_shape=(pltpu.VMEM((height, width), kind), *begun),
        in_specs=[pl.BlockSpec(memory_space=pltpu.HBM), pl.BlockSpec(memory_space=pltpu.SMEM)],
        out_specs=(pl.BlockSpec(memory_space=pltpu.VMEM),) + (pl.BlockSpec(memory_space=pltpu.HBM),) * 2,
        scratch_shapes=[pltpu.SemaphoreType.DMA((4,))],
        compiler_params=pltpu.CompilerParams(vmem_limit_bytes=8 * MIB),
    )(pltpu.with_memory_space_constraint(orbitals, pltpu.HBM), tally)
    held["across", 0] = send(first, across)
    held["across", 1] = send(second, across)
    beside = send(own, sibling)
    near = after(kern_near, own)
    square = jax.ShapeDtypeStruct((height, height), kind)
    down0, down1, up0, up1 = call(
        prepare_body, (square,) * 4, [near[:, 0, :], near[:, 1, :], couple], smem=1
    )
    held["total"] = call(
        diagonal_body, pltpu.VMEM((height, width), jnp.float32), [own, after(kern_diag, up0)],
        scratch=[pltpu.VMEM((height, height), kind)], flops=4 * height * height * width,
    )

    depth = height + 3 * (height - sum(CUTS[-HOLD:]))

    def collect(base, pieces):
        state = [held[n] for n in ("rows", "gram") if n in held]
        args = [own, *pieces] + state
        out = (pltpu.VMEM((depth, width), kind), pltpu.VMEM((depth, height), jnp.float32))
        aliases = {len(args) - 2: 0, len(args) - 1: 1} if state else {}
        count = sum(p.shape[0] for p in pieces)
        held["rows"], held["gram"] = call(
            functools.partial(collect_body, len(pieces), base), out, args, aliases=aliases,
            flops=2 * count * height * width,
        )

    join(("across", 0), "total")
    def swap(i):
        held["swap", i] = send(jnp.where(mixed, held["across", i], held["onward", i]), sibling)

    def collected(i):
        collect(height + 3 * spans[i].start, pieces(i))

    swaps = collects = 0
    for w in range(1, last + 1):
        now = held["total"]
        if w + 1 <= last:
            held["across", w + 1] = send(part(w + 1, now), across)
        held["onward", w - 1] = send(held["across", w - 1], onward)
        if w == KAT:
            for o, down in ((1, down1), (0, down0)):
                pairs = [(i, i + o + 1) for i in range(peers - o - 1)]
                held["down", o] = send(after(down, now), pairs)
        if w >= LAG:
            swap(w - LAG)
        if w == LAG:
            collect(0, [after(beside, held["total"])])
        if w >= LAG + 1:
            collected(w - LAG - 1)
        join(("across", w), ("onward", w - LAG + 1), ("swap", w - LAG), "rows", "gram", "total")
    held["onward", last] = send(held["across", last], onward)
    if KAT > last:
        for o, down in ((1, down1), (0, down0)):
            pairs = [(i, i + o + 1) for i in range(peers - o - 1)]
            held["down", o] = send(after(down, held["rows"]), pairs)
    kept = last + 1 - HOLD
    for i in range(last - LAG + 1, kept):
        swap(i)
    join(("onward", last - 1), "rows", "gram")
    for i in range(last - LAG, kept):
        collected(i)
    gate = [("onward", i) for i in range(kept, last + 1)]
    join(*gate, "rows", "gram")
    for i in range(kept, last + 1):
        swap(i)
    kerns = [held["down", 0], held["down", 1], up0, up1]
    held["total"] = call(
        functools.partial(product_body, spans[:kept]), pltpu.VMEM((height, width), jnp.float32),
        [held["gram"], held["rows"], *kerns, held["total"], place], smem=1, aliases={6: 0},
        scratch=[pltpu.VMEM((depth, height), kind)], flops=2 * depth * height * width,
    )
    count = 3 * (height - spans[kept].start)
    final = [held[n, i] for n in ("across", "onward", "swap") for i in range(kept, last + 1)]
    return call(
        functools.partial(last_body, slice(spans[kept].start, height), len(final)),
        jax.ShapeDtypeStruct((height, width), kind),
        [own, *final, *kerns, held["total"], place], smem=1, out_hbm=True,
        scratch=[
            pltpu.VMEM((count, width), kind), pltpu.VMEM((height, count), kind), pltpu.VMEM((height, width), kind),
            pltpu.SemaphoreType.DMA((width // TILE,)),
        ],
        limit=16, flops=4 * count * height * width,
    )


def solution(mesh):
    placed = (
        P(("groups", "pts"), None),
        P(("groups", "pts"), None),
        P(("groups", "pts"), None, None),
        P(("groups", "pts"), None),
        P(("groups", "pts")),
    )
    return jax.shard_map(
        on_device, mesh=mesh, in_specs=placed, out_specs=P(("groups", "pts"), None), check_vma=False
    )
```
